32 devices in a mesh: grp: 2 (over y), mom: 16 (over z, x, core).
Axes of the slice: x: 2, y: 2, z: 4, core: 2. Of those that a mesh axis runs over, the one named last changes fastest.
Arguments:
- green_function: bfloat16 [2, 4096, 512], P(None, ('grp', 'mom')), parts along dimension 1, may hold values from -0.8984375 to 0.8984375
- couplings: bfloat16 [8, 2, 512, 512], replicated, may hold values from -0.1875 to 0.1875
- phonon_modes: int32 [3, 4], replicated, may hold values from 0 to 7
- weights: float32 [3, 4], replicated, may hold values from 0.5 to 2
Outputs:
- self_energy: float32 [2, 4096, 512], P(None, ('grp', 'mom')), parts along dimension 1
The draws below stay inside these ranges and needn't reach their ends.
There are 2 independent parts, one for each index of `grp`. The reference program is written for one: setup_inputs(seed, part) draws one part's arguments, and reference() takes and returns one part's arrays. A program takes and returns all parts, laid end to end along the dimension named above; an argument that names none is the same for every part. Nothing has to cross between parts.
Inputs may be any that keep to these rules, and one draw needn't show every extreme that they name: `phonon_modes`: each entry names one matrix of couplings.
All inputs are finite; a program needn't handle non-finite values.
Results may differ from the reference program's by a relative error of at most 0.0042.
Values may be sent and summed in bfloat16 or wider, within the bound.
A program may use at most 64 MiB of HBM per device.

```python
import math
import jax
import jax.numpy as jnp
from jax import lax

SLAB = 512
NK = 4
ROWS = 2048
HALF = 1
STOPS = 3
MODES = 4
BANK = 8


def set_ends(drawn, own_key, smallest, high):
    longest = drawn.shape.index(max(drawn.shape))
    spots = []
    for shift in (0, 1):
        where = [jax.random.randint(jax.random.fold_in(own_key, axis), (), 0, length) for axis, length in enumerate(drawn.shape)]
        where[longest] = (where[longest] + shift) % drawn.shape[longest]
        spots.append(tuple(where))
    return drawn.at[spots[0]].set(smallest).at[spots[1]].set(high)


def block_scale(own_key, dims, pieces, smallest, largest):
    gain = 1.0
    for position, parts in pieces:
        draws = jax.random.uniform(jax.random.fold_in(jax.random.fold_in(own_key, 6), position), (parts,), jnp.float32, smallest / len(pieces), largest / len(pieces))
        gain = gain * jnp.repeat(jnp.exp(draws), dims[position] // parts).reshape((-1,) + (1,) * (len(dims) - 1 - position))
    return gain


def normal_values(key, shape, deviation, most, shards=(), kind=jnp.bfloat16):
    values = deviation * jax.random.normal(key, shape, jnp.float32)
    if shards:
        values = values * block_scale(key, shape, shards, -0.22, 0.18)
    return jnp.clip(values, -most, most).astype(kind)


def setup_inputs(seed: int = 0, part: int = 0) -> dict:
    seeds = jax.random.split(jax.random.key(seed), 5)
    part_keys = jax.random.split(jax.random.fold_in(seeds[4], part), 5)
    return {
        "green_function": normal_values(part_keys[0], (2, ROWS, SLAB), 0.15, 0.8984375, ((1, 16),)),
        "couplings": normal_values(seeds[1], (BANK, 2, SLAB, SLAB), (2 * SLAB) ** -0.5, 0.1875),
        "phonon_modes": set_ends(jax.random.randint(seeds[2], (STOPS, MODES), 0, BANK), jax.random.fold_in(seeds[2], 1), 0, BANK - 1).astype(jnp.int32),
        "weights": jnp.clip(jnp.exp(jax.random.uniform(seeds[3], (STOPS, MODES), jnp.float32, math.log(0.5), math.log(2.0))), 0.5, 2.0),
    }


def spectral_of(green_block):
    real_part = green_block[0].astype(jnp.float32)
    imag_part = green_block[1].astype(jnp.float32)
    spec_real = -(imag_part + imag_part.T)
    spec_imag = real_part - real_part.T
    return jnp.stack([spec_real, spec_imag]).astype(jnp.bfloat16)


def stack_spectral(spectral):
    upper_half = jnp.concatenate([spectral[0], spectral[1]], axis=1)
    lower_half = jnp.concatenate([-spectral[1], spectral[0]], axis=1)
    return jnp.concatenate([upper_half, lower_half], axis=0)


def stack_coupling(coupling):
    upper_half = jnp.concatenate([coupling[0], coupling[1]], axis=1)
    lower_half = jnp.concatenate([-coupling[1], coupling[0]], axis=1)
    return jnp.concatenate([upper_half, lower_half], axis=0)


def reference(green_function, couplings, phonon_modes, weights):
    blocks = green_function.reshape(2, NK, SLAB, SLAB).transpose(1, 0, 2, 3)
    spectra = lax.map(spectral_of, blocks)

    def one_momentum(momentum):
        accumulated = jnp.zeros((SLAB, 2 * SLAB), jnp.float32)
        for stop_index in range(STOPS):
            source = (momentum + HALF - stop_index) % NK
            spectral = lax.dynamic_index_in_dim(spectra, source.astype(jnp.int32), 0, keepdims=False)
            stacked = stack_spectral(spectral)
            for mode_index in range(MODES):
                coupling = lax.dynamic_index_in_dim(couplings, phonon_modes[stop_index, mode_index], 0, keepdims=False)
                left_rows = jnp.concatenate([coupling[0], coupling[1]], axis=1)
                product = jnp.dot(left_rows, stacked, preferred_element_type=jnp.float32).astype(jnp.bfloat16)
                right_side = stack_coupling(coupling)
                contribution = lax.dot_general(product, right_side, (((1,), (1,)), ((), ())), preferred_element_type=jnp.float32)
                accumulated = accumulated + weights[stop_index, mode_index] * contribution
        return accumulated

    self_energy = lax.map(one_momentum, jnp.arange(NK, dtype=jnp.int32))
    return self_energy.reshape(NK, SLAB, 2, SLAB).transpose(2, 0, 1, 3).reshape(2, NK * SLAB, SLAB)
```

```python
import functools

import jax
import jax.numpy as jnp
from jax import lax
from jax.experimental import pallas as pl
from jax.experimental.pallas import tpu as pltpu
from jax.sharding import PartitionSpec as P

MESH = pl.DeviceIdType.MESH
NT = (((1,), (1,)), ((), ()))


def kernel(
    dims, green, couplings, modes, weights, out,
    gathered, bank, left, rows_stack, product, own, outgoing, incoming,
    own_sem, bank_sem, pair_sems, chip_sems, relay_sems, term_sems,
):
    mom_size, group, tile, order, bank_size, stops, mode_count, chunk = dims
    reach = (stops - 1) // 2
    chips = group // 2
    me = lax.axis_index("mom")
    member = lax.rem(me, group)
    base = me - member
    core = lax.rem(member, 2)
    chip = member // 2
    mate = base + member + 1 - 2 * core

    def at(position):
        return {"mom": position}

    others = [base + lax.rem(chip + d, chips) * 2 + core for d in range(1, chips)]
    shifts = [s for s in range(stops) if s != reach]
    targets = [lax.rem(me + (s - reach) * group + mom_size, mom_size) for s in shifts]

    own_copy = pltpu.make_async_copy(green, gathered.at[member], own_sem)
    own_copy.start()
    loads = []
    for b in range(bank_size):
        for part in range(2):
            load = pltpu.make_async_copy(
                couplings.at[b, part],
                bank.at[b, :, pl.ds(part * order, order)],
                bank_sem.at[b, part],
            )
            load.start()
            loads.append(load)

    barrier = pltpu.get_barrier_semaphore()
    neighbours = [mate] + others + targets
    for neighbour in neighbours:
        pl.semaphore_signal(barrier, inc=1, device_id=at(neighbour), device_id_type=MESH)
    pl.semaphore_wait(barrier, len(neighbours))

    def remote(src, dst, sems, to):
        return pltpu.make_async_remote_copy(
            src_ref=src, dst_ref=dst, send_sem=sems.at[0], recv_sem=sems.at[1],
            device_id=at(to), device_id_type=MESH,
        )

    chip_copies = []
    for part in range(2):
        for d, other in enumerate(others):
            copy = remote(
                green.at[part], gathered.at[member, part], chip_sems.at[d, part], other
            )
            copy.start()
            chip_copies.append((d, part, copy))
    pair_copy = remote(green, gathered.at[member], pair_sems, mate)
    pair_copy.start()
    relays = []
    for d, part, copy in chip_copies:
        source = lax.rem(chip + chips - (d + 1), chips) * 2 + core
        copy.wait_recv()
        relay = remote(
            gathered.at[source, part], gathered.at[source, part], relay_sems.at[d, part], mate
        )
        relay.start()
        relays.append(relay)

    scale = [
        [
            sum(
                jnp.where(modes[s, m] == b, weights[s, m], jnp.float32(0.0))
                for m in range(mode_count)
            )
            for b in range(bank_size)
        ]
        for s in range(stops)
    ]
    for load in loads:
        load.wait()
    for b in range(bank_size):
        left[pl.ds(b * tile, tile), :] = bank[b, pl.ds(pl.multiple_of(member * tile, tile), tile), :]
    own_copy.wait()
    pair_copy.wait_recv()
    for relay in relays:
        relay.wait_recv()

    for j in range(group):
        columns = pl.ds(j * tile, tile)
        mirror = [
            jnp.concatenate(
                [gathered[i, part, :, columns].T for i in range(group)], axis=1
            ).astype(jnp.float32)
            for part in range(2)
        ]
        spec_real = -(gathered[j, 1].astype(jnp.float32) + mirror[1])
        spec_imag = gathered[j, 0].astype(jnp.float32) - mirror[0]
        spec_real = spec_real.astype(jnp.bfloat16)
        spec_imag = spec_imag.astype(jnp.bfloat16)
        rows_stack[pl.ds(2 * j * tile, tile), pl.ds(0, order)] = spec_real
        rows_stack[pl.ds(2 * j * tile, tile), pl.ds(order, order)] = spec_imag
        rows_stack[pl.ds((2 * j + 1) * tile, tile), pl.ds(0, order)] = -spec_imag
        rows_stack[pl.ds((2 * j + 1) * tile, tile), pl.ds(order, order)] = spec_real
        both = lax.dot_general(
            left[...], rows_stack[pl.ds(2 * j * tile, 2 * tile), :], NT,
            preferred_element_type=jnp.float32,
        ).astype(jnp.bfloat16)
        for b in range(bank_size):
            block = both[b * tile : (b + 1) * tile]
            real, imag = block[:, :tile], block[:, tile:]
            product[b, pl.ds(0, tile), pl.ds(j * tile, tile)] = real
            product[b, pl.ds(0, tile), pl.ds(order + j * tile, tile)] = imag
            product[b, pl.ds(tile, tile), pl.ds(j * tile, tile)] = imag
            product[b, pl.ds(tile, tile), pl.ds(order + j * tile, tile)] = -real

    term_copies = []
    for c in range(order // chunk):
        terms = [
            lax.dot_general(
                product[b], bank[b, pl.ds(c * chunk, chunk), :], NT,
                preferred_element_type=jnp.float32,
            )
            for b in range(bank_size)
        ]
        for index, s in enumerate(shifts):
            outgoing[index, c] = sum(
                scale[s][b] * terms[b] for b in range(bank_size)
            ).astype(jnp.bfloat16)
            copy = remote(
                outgoing.at[index, c], incoming.at[index, c], term_sems.at[index, c],
                targets[index],
            )
            copy.start()
            term_copies.append(copy)
        own[c] = sum(scale[reach][b] * terms[b] for b in range(bank_size))

    for c in range(order // chunk):
        total = own[c]
        for index in range(len(shifts)):
            term_copies[c * len(shifts) + index].wait_recv()
            total = total + incoming[index, c].astype(jnp.float32)
        out[0, :, pl.ds(c * chunk, chunk)] = total[:tile]
        out[1, :, pl.ds(c * chunk, chunk)] = total[tile:]

    for _, _, copy in chip_copies:
        copy.wait_send()
    pair_copy.wait_send()
    for relay in relays:
        relay.wait_send()
    for copy in term_copies:
        copy.wait_send()


def body(green_function, couplings, phonon_modes, weights):
    _, tile, order = green_function.shape
    group = order // tile
    chips = group // 2
    bank_size = couplings.shape[0]
    stops, mode_count = phonon_modes.shape
    mom_size = lax.axis_size("mom")
    chunk = min(2 * tile, order)
    chunks = order // chunk
    dims = (mom_size, group, tile, order, bank_size, stops, mode_count, chunk)
    bf16, f32 = jnp.bfloat16, jnp.float32
    flops = 8 * bank_size * tile * order * order * 2
    return pl.pallas_call(
        functools.partial(kernel, dims),
        out_shape=jax.ShapeDtypeStruct((2, tile, order), f32),
        in_specs=[
            pl.BlockSpec(memory_space=pl.ANY),
            pl.BlockSpec(memory_space=pl.ANY),
            pl.BlockSpec(memory_space=pltpu.SMEM),
            pl.BlockSpec(memory_space=pltpu.SMEM),
        ],
        out_specs=pl.BlockSpec(memory_space=pltpu.VMEM),
        scratch_shapes=[
            pltpu.VMEM((group, 2, tile, order), bf16),
            pltpu.VMEM((bank_size, order, 2 * order), bf16),
            pltpu.VMEM((bank_size * tile, 2 * order), bf16),
            pltpu.VMEM((2 * order, 2 * order), bf16),
            pltpu.VMEM((bank_size, 2 * tile, 2 * order), bf16),
            pltpu.VMEM((chunks, 2 * tile, chunk), f32),
            pltpu.VMEM((stops - 1, chunks, 2 * tile, chunk), bf16),
            pltpu.VMEM((stops - 1, chunks, 2 * tile, chunk), bf16),
            pltpu.SemaphoreType.DMA,
            pltpu.SemaphoreType.DMA((bank_size, 2)),
            pltpu.SemaphoreType.DMA((2,)),
            pltpu.SemaphoreType.DMA((max(chips - 1, 1), 2, 2)),
            pltpu.SemaphoreType.DMA((max(chips - 1, 1), 2, 2)),
            pltpu.SemaphoreType.DMA((stops - 1, chunks, 2)),
        ],
        compiler_params=pltpu.CompilerParams(
            collective_id=0, has_side_effects=True, vmem_limit_bytes=48 * 2**20
        ),
        cost_estimate=pl.CostEstimate(flops=flops, bytes_accessed=10 * 2**20, transcendentals=0),
    )(green_function, couplings, phonon_modes, weights)


def solution(mesh):
    in_specs = (P(None, ("grp", "mom"), None), P(), P(), P())
    out_specs = P(None, ("grp", "mom"), None)
    return jax.shard_map(body, mesh=mesh, in_specs=in_specs, out_specs=out_specs, check_vma=False)
```

```python
import functools

import jax
import jax.numpy as jnp
from jax import lax
from jax.experimental import pallas as pl
from jax.experimental.pallas import tpu as pltpu
from jax.sharding import PartitionSpec as P

MESH = pl.DeviceIdType.MESH
NT = (((1,), (1,)), ((), ()))


def kernel(
    dims, green, couplings, modes_hbm, weights_hbm, out,
    modes, weights, gathered, bank, left, rows_stack, product,
    own, outgoing, incoming, mate_incoming, mirror_out, mirror_in,
    small_sems, bank_sem, pair_sems, chip_sems, relay_sems, term_sems, mate_term_sems,
    mirror_sems,
):
    mom_size, group, tile, order, bank_size, stops, mode_count = dims
    f32, bf16 = jnp.float32, jnp.bfloat16
    reach = (stops - 1) // 2
    chips = group // 2
    wide = 2 * tile
    me = lax.axis_index("mom")
    member = lax.rem(me, group)
    base = me - member
    core = lax.rem(member, 2)
    chip = member // 2
    mate = base + chip * 2 + 1 - core

    def at(position):
        return {"mom": position}

    def remote(src, dst, send, recv, to):
        return pltpu.make_async_remote_copy(
            src_ref=src, dst_ref=dst, send_sem=send, recv_sem=recv,
            device_id=at(to), device_id_type=MESH,
        )

    def columns_of(chip_index):
        return pl.ds(pl.multiple_of(chip_index * wide, wide), wide)

    shifts = [s for s in range(stops) if s != reach]
    targets = [lax.rem(me + (s - reach) * group + mom_size, mom_size) for s in shifts]

    own_copy = pltpu.make_async_copy(green, gathered.at[member], small_sems.at[0])
    own_copy.start()
    small = [
        pltpu.make_async_copy(modes_hbm, modes, small_sems.at[1]),
        pltpu.make_async_copy(weights_hbm, weights, small_sems.at[2]),
    ]
    for copy in small:
        copy.start()
    loads = []
    for b in range(bank_size):
        for part in range(2):
            load = pltpu.make_async_copy(
                couplings.at[b, part],
                bank.at[b, :, pl.ds(part * order, order)],
                bank_sem.at[b, part],
            )
            load.start()
            loads.append(load)

    barrier = pltpu.get_barrier_semaphore()
    neighbours = [base + lax.rem(member + d, group) for d in range(1, group)] + targets
    for neighbour in neighbours:
        pl.semaphore_signal(barrier, inc=1, device_id=at(neighbour), device_id_type=MESH)
    pl.semaphore_wait(barrier, len(neighbours))

    chip_copies = {}
    for e in range(chips):
        for d in range(1, chips):
            other = lax.rem(chip + d, chips)
            columns = columns_of(lax.rem(other + e, chips))
            copy = remote(
                green.at[:, :, columns], gathered.at[member, :, :, columns],
                chip_sems.at[e, d, 0], chip_sems.at[e, d, 1], base + other * 2 + core,
            )
            copy.start()
            chip_copies[e, d] = copy
    pair_copy = remote(green, gathered.at[member], pair_sems.at[0], pair_sems.at[1], mate)
    pair_copy.start()

    relays = []

    def collect(e):
        latest = []
        for d in range(1, chips):
            source = lax.rem(chip + chips - d, chips) * 2 + core
            columns = columns_of(lax.rem(chip + e, chips))
            chip_copies[e, d].wait_recv()
            relay = remote(
                gathered.at[source, :, :, columns], gathered.at[source, :, :, columns],
                relay_sems.at[e, d, 0], relay_sems.at[e, d, 1], mate,
            )
            relay.start()
            latest.append(relay)
        relays.extend(latest)
        return latest

    def first_products(chip_index):
        for half in range(2):
            j = chip_index * 2 + half
            columns = pl.ds(pl.multiple_of(j * tile, tile), tile)
            beyond = pl.ds(pl.multiple_of(order + j * tile, tile), tile)
            mirror = [
                jnp.concatenate(
                    [gathered[i, part, :, columns].T for i in range(group)], axis=1
                ).astype(f32)
                for part in range(2)
            ]
            spec_real = (-(gathered[j, 1].astype(f32) + mirror[1])).astype(bf16)
            spec_imag = (gathered[j, 0].astype(f32) - mirror[0]).astype(bf16)
            rows_stack[half, pl.ds(0, tile), pl.ds(0, order)] = spec_real
            rows_stack[half, pl.ds(0, tile), pl.ds(order, order)] = spec_imag
            rows_stack[half, pl.ds(tile, tile), pl.ds(0, order)] = -spec_imag
            rows_stack[half, pl.ds(tile, tile), pl.ds(order, order)] = spec_real
            both = lax.dot_general(
                left[...], rows_stack[half], NT, preferred_element_type=f32
            ).astype(bf16)
            for b in range(bank_size):
                block = both[b * tile : (b + 1) * tile]
                real, imag = block[:, :tile], block[:, tile:]
                product[b, pl.ds(0, tile), columns] = real
                product[b, pl.ds(0, tile), beyond] = imag
                product[b, pl.ds(tile, tile), columns] = imag
                product[b, pl.ds(tile, tile), beyond] = -real

    for copy in small:
        copy.wait()
    scale = [
        [
            sum(
                jnp.where(modes[s, m] == b, weights[s, m], jnp.float32(0.0))
                for m in range(mode_count)
            )
            for b in range(bank_size)
        ]
        for s in range(stops)
    ]
    for load in loads:
        load.wait()
    for b in range(bank_size):
        left[pl.ds(b * tile, tile), :] = bank[b, pl.ds(pl.multiple_of(member * tile, tile), tile), :]

    own_copy.wait()
    latest = collect(0)
    pair_copy.wait_recv()
    for relay in latest:
        relay.wait_recv()
    first_products(chip)
    waits = []
    for e in range(1, chips):
        waits += collect(e)
    for relay in waits:
        relay.wait_recv()
    for e in range(1, chips):
        first_products(lax.rem(chip + e, chips))

    def chosen(d):
        other = lax.rem(chip + d, chips)
        later = jnp.where(other > chip, 1, 0)
        return other, core * later + (1 - core) * (1 - later)

    def second_products(d):
        other, pick = chosen(d)
        rows = columns_of(other)
        terms = [
            lax.dot_general(product[b], bank[b, rows, :], NT, preferred_element_type=f32)
            for b in range(bank_size)
        ]
        for index, s in enumerate(shifts):
            combined = sum(scale[s][b] * terms[b] for b in range(bank_size)).astype(bf16)
            outgoing[index, d, 0] = combined[:, :tile]
            outgoing[index, d, 1] = combined[:, tile:]
            term_copy(index, d).start()
            if d == 0:
                @pl.when(core == 0)
                def _():
                    mate_copy(index).start()
        combined = sum(scale[reach][b] * terms[b] for b in range(bank_size))
        own[d, 0] = combined[:, :tile]
        own[d, 1] = combined[:, tile:]

    def term_copy(index, d):
        pick = core if d == 0 else chosen(d)[1]
        return remote(
            outgoing.at[index, d, pick], incoming.at[index, d],
            term_sems.at[index, d, 0], term_sems.at[index, d, 1], targets[index],
        )

    def mate_copy(index):
        return remote(
            outgoing.at[index, 0, 1], mate_incoming.at[index],
            mate_term_sems.at[index, 0], mate_term_sems.at[index, 1], targets[index],
        )

    def mirror_copy(d):
        to = mate if d == 0 else base + chosen(d)[0] * 2 + chosen(d)[1]
        return remote(
            mirror_out.at[d], mirror_in.at[d], mirror_sems.at[d, 0], mirror_sems.at[d, 1], to
        )

    def received(d):
        total = None
        for index in range(len(shifts)):
            term_copy(index, d).wait_recv()
            piece = incoming[index, d].astype(f32)
            total = piece if total is None else total + piece
        return total

    def put(j, value):
        columns = pl.ds(pl.multiple_of(j * tile, tile), tile)
        out[0, :, columns] = value[:tile]
        out[1, :, columns] = value[tile:]

    def mirrored(d):
        block = mirror_in[d]
        return jnp.concatenate([block[:tile].T.astype(f32), -block[tile:].T.astype(f32)], axis=0)

    for d in list(range(1, chips)) + [0]:
        second_products(d)
    for d in range(1, chips):
        other, pick = chosen(d)
        total = received(d)
        mirror_out[d] = total.astype(bf16)
        mirror_copy(d).start()
        put(other * 2 + pick, own[d, pick] + total)

    @pl.when(core == 0)
    def _():
        total = None
        for index in range(len(shifts)):
            mate_copy(index).wait_recv()
            piece = mate_incoming[index].astype(f32)
            total = piece if total is None else total + piece
        mirror_out[0] = total.astype(bf16)
        mirror_copy(0).start()
        put(chip * 2 + 1, own[0, 1] + total)

    for d in range(1, chips):
        source = lax.rem(chip + chips - d, chips)
        slot = chips - d
        same = jnp.where(source < chip, 1, 0)
        which = core * same + (1 - core) * (1 - same)
        mirror_copy(d).wait_recv()
        put(source * 2 + which, own[slot, which] + mirrored(d))

    put(member, own[0, core] + received(0))

    @pl.when(core == 1)
    def _():
        mirror_copy(0).wait_recv()
        put(chip * 2, own[0, 0] + mirrored(0))

    for copy in chip_copies.values():
        copy.wait_send()
    pair_copy.wait_send()
    for relay in relays:
        relay.wait_send()
    for index in range(len(shifts)):
        for d in range(chips):
            term_copy(index, d).wait_send()
    for d in range(1, chips):
        mirror_copy(d).wait_send()

    @pl.when(core == 0)
    def _():
        for index in range(len(shifts)):
            mate_copy(index).wait_send()
        mirror_copy(0).wait_send()


def body(green_function, couplings, phonon_modes, weights):
    _, tile, order = green_function.shape
    group = order // tile
    chips = group // 2
    bank_size = couplings.shape[0]
    stops, mode_count = phonon_modes.shape
    dims = (lax.axis_size("mom"), group, tile, order, bank_size, stops, mode_count)
    bf16, f32 = jnp.bfloat16, jnp.float32
    flops = 8 * bank_size * tile * order * order * 2
    dma = pltpu.SemaphoreType.DMA
    return pl.pallas_call(
        functools.partial(kernel, dims),
        out_shape=jax.ShapeDtypeStruct((2, tile, order), f32),
        in_specs=[pl.BlockSpec(memory_space=pltpu.HBM)] * 4,
        out_specs=pl.BlockSpec(memory_space=pltpu.VMEM),
        scratch_shapes=[
            pltpu.SMEM((stops, mode_count), jnp.int32),
            pltpu.SMEM((stops, mode_count), f32),
            pltpu.VMEM((group, 2, tile, order), bf16),
            pltpu.VMEM((bank_size, order, 2 * order), bf16),
            pltpu.VMEM((bank_size * tile, 2 * order), bf16),
            pltpu.VMEM((2, 2 * tile, 2 * order), bf16),
            pltpu.VMEM((bank_size, 2 * tile, 2 * order), bf16),
            pltpu.VMEM((chips, 2, 2 * tile, tile), f32),
            pltpu.VMEM((stops - 1, chips, 2, 2 * tile, tile), bf16),
            pltpu.VMEM((stops - 1, chips, 2 * tile, tile), bf16),
            pltpu.VMEM((stops - 1, 2 * tile, tile), bf16),
            pltpu.VMEM((chips, 2 * tile, tile), bf16),
            pltpu.VMEM((chips, 2 * tile, tile), bf16),
            dma((3,)),
            dma((bank_size, 2)),
            dma((2,)),
            dma((chips, chips, 2)),
            dma((chips, chips, 2)),
            dma((stops - 1, chips, 2)),
            dma((stops - 1, 2)),
            dma((chips, 2)),
        ],
        compiler_params=pltpu.CompilerParams(
            collective_id=0, has_side_effects=True, vmem_limit_bytes=63 * 2**20
        ),
        cost_estimate=pl.CostEstimate(flops=flops, bytes_accessed=10 * 2**20, transcendentals=0),
    )(green_function, couplings, phonon_modes, weights)


def solution(mesh):
    in_specs = (P(None, ("grp", "mom"), None), P(), P(), P())
    out_specs = P(None, ("grp", "mom"), None)
    return jax.shard_map(body, mesh=mesh, in_specs=in_specs, out_specs=out_specs, check_vma=False)
```

```python
import functools

import jax
import jax.numpy as jnp
from jax import lax
from jax.experimental import pallas as pl
from jax.experimental.pallas import tpu as pltpu
from jax.sharding import PartitionSpec as P

MESH = pl.DeviceIdType.MESH
NT = (((1,), (1,)), ((), ()))


def kernel(
    dims, green, couplings, modes_hbm, weights_hbm, out,
    modes, weights, gathered, bank, left, mirrors, rows_stack, product,
    own, outgoing, incoming, packed_out, packed_in, mate_incoming, mirror_out, mirror_in,
    small_sems, bank_sem, pair_sems, chip_sems, relay_sems, term_sems, mate_term_sems,
    mirror_sems,
):
    mom_size, group, tile, order, bank_size, stops, mode_count = dims
    f32, bf16 = jnp.float32, jnp.bfloat16
    reach = (stops - 1) // 2
    chips = group // 2
    wide = 2 * tile
    me = lax.axis_index("mom")
    member = lax.rem(me, group)
    base = me - member
    core = lax.rem(member, 2)
    chip = member // 2
    mate = base + chip * 2 + 1 - core

    def at(position):
        return {"mom": position}

    def remote(src, dst, send, recv, to):
        return pltpu.make_async_remote_copy(
            src_ref=src, dst_ref=dst, send_sem=send, recv_sem=recv,
            device_id=at(to), device_id_type=MESH,
        )

    def columns_of(chip_index):
        return pl.ds(pl.multiple_of(chip_index * wide, wide), wide)

    shifts = [s for s in range(stops) if s != reach]
    targets = [lax.rem(me + (s - reach) * group + mom_size, mom_size) for s in shifts]

    own_copy = pltpu.make_async_copy(green, gathered.at[member], small_sems.at[0])
    own_copy.start()
    small = [
        pltpu.make_async_copy(modes_hbm, modes, small_sems.at[1]),
        pltpu.make_async_copy(weights_hbm, weights, small_sems.at[2]),
    ]
    for copy in small:
        copy.start()
    loads = []
    for b in range(bank_size):
        for part in range(2):
            load = pltpu.make_async_copy(
                couplings.at[b, part],
                bank.at[b, :, pl.ds(part * order, order)],
                bank_sem.at[b, part],
            )
            load.start()
            loads.append(load)

    barrier = pltpu.get_barrier_semaphore()
    neighbours = [base + lax.rem(member + d, group) for d in range(1, group)] + targets
    for neighbour in neighbours:
        pl.semaphore_signal(barrier, inc=1, device_id=at(neighbour), device_id_type=MESH)
    pl.semaphore_wait(barrier, len(neighbours))

    chip_copies = {}
    for e in range(chips):
        for d in range(1, chips):
            other = lax.rem(chip + d, chips)
            columns = columns_of(lax.rem(other + e, chips))
            copy = remote(
                green.at[:, :, columns], gathered.at[member, :, :, columns],
                chip_sems.at[e, d, 0], chip_sems.at[e, d, 1], base + other * 2 + core,
            )
            copy.start()
            chip_copies[e, d] = copy
    pair_copy = remote(green, gathered.at[member], pair_sems.at[0], pair_sems.at[1], mate)
    pair_copy.start()

    relays = []

    def collect(e):
        latest = []
        for d in range(1, chips):
            source = lax.rem(chip + chips - d, chips) * 2 + core
            columns = columns_of(lax.rem(chip + e, chips))
            chip_copies[e, d].wait_recv()
            relay = remote(
                gathered.at[source, :, :, columns], gathered.at[source, :, :, columns],
                relay_sems.at[e, d, 0], relay_sems.at[e, d, 1], mate,
            )
            relay.start()
            latest.append(relay)
        relays.extend(latest)
        return latest

    def mirror_tiles(column_chip, row_chip):
        for half in range(2):
            columns = pl.ds(pl.multiple_of((column_chip * 2 + half) * tile, tile), tile)
            for lane in range(2):
                i = row_chip * 2 + lane
                place = pl.ds(pl.multiple_of(i * tile, tile), tile)
                for part in range(2):
                    mirrors[half, part, :, place] = gathered[i, part, :, columns].T

    def first_products(chip_index):
        for half in range(2):
            j = chip_index * 2 + half
            columns = pl.ds(pl.multiple_of(j * tile, tile), tile)
            beyond = pl.ds(pl.multiple_of(order + j * tile, tile), tile)
            spec_real = (-(gathered[j, 1].astype(f32) + mirrors[half, 1].astype(f32))).astype(bf16)
            spec_imag = (gathered[j, 0].astype(f32) - mirrors[half, 0].astype(f32)).astype(bf16)
            rows_stack[half, pl.ds(0, tile), pl.ds(0, order)] = spec_real
            rows_stack[half, pl.ds(0, tile), pl.ds(order, order)] = spec_imag
            rows_stack[half, pl.ds(tile, tile), pl.ds(0, order)] = -spec_imag
            rows_stack[half, pl.ds(tile, tile), pl.ds(order, order)] = spec_real
            both = lax.dot_general(
                left[...], rows_stack[half], NT, preferred_element_type=f32
            ).astype(bf16)
            for b in range(bank_size):
                block = both[b * tile : (b + 1) * tile]
                real, imag = block[:, :tile], block[:, tile:]
                product[b, pl.ds(0, tile), columns] = real
                product[b, pl.ds(0, tile), beyond] = imag
                product[b, pl.ds(tile, tile), columns] = imag
                product[b, pl.ds(tile, tile), beyond] = -real

    for copy in small:
        copy.wait()
    scale = [
        [
            sum(
                jnp.where(modes[s, m] == b, weights[s, m], jnp.float32(0.0))
                for m in range(mode_count)
            )
            for b in range(bank_size)
        ]
        for s in range(stops)
    ]
    for load in loads:
        load.wait()
    for b in range(bank_size):
        left[pl.ds(b * tile, tile), :] = bank[b, pl.ds(pl.multiple_of(member * tile, tile), tile), :]

    own_copy.wait()
    pair_copy.wait_recv()
    mirror_tiles(chip, chip)
    latest = collect(0)
    for relay in latest:
        relay.wait_recv()
    for e in range(1, chips):
        mirror_tiles(chip, lax.rem(chip + e, chips))
    first_products(chip)
    waits = []
    if chips == 2:
        mirror_tiles(1 - chip, chip)
    for e in range(1, chips):
        waits += collect(e)
    for relay in waits:
        relay.wait_recv()
    for e in range(1, chips):
        column_chip = lax.rem(chip + e, chips)
        for d in range(1 if chips == 2 else 0, chips):
            mirror_tiles(column_chip, lax.rem(chip + d, chips))
        first_products(column_chip)

    def chosen(d):
        other = lax.rem(chip + d, chips)
        later = jnp.where(other > chip, 1, 0)
        return other, core * later + (1 - core) * (1 - later)

    upper = lax.broadcasted_iota(jnp.int32, (tile, tile), 0) <= lax.broadcasted_iota(
        jnp.int32, (tile, tile), 1
    )

    def second_products(d):
        other, pick = chosen(d)
        rows = columns_of(other)
        terms = [
            lax.dot_general(product[b], bank[b, rows, :], NT, preferred_element_type=f32)
            for b in range(bank_size)
        ]
        for index, s in enumerate(shifts):
            combined = sum(scale[s][b] * terms[b] for b in range(bank_size))
            outgoing[index, d, 0] = combined[:, :tile].astype(bf16)
            outgoing[index, d, 1] = combined[:, tile:].astype(bf16)
            if d == 0:
                half = jnp.where(core == 0, combined[:, :tile], combined[:, tile:])
                packed_out[index] = jnp.where(upper, half[:tile], half[tile:]).astype(bf16)
            term_copy(index, d).start()
            if d == 0:
                @pl.when(core == 0)
                def _():
                    mate_copy(index).start()
        combined = sum(scale[reach][b] * terms[b] for b in range(bank_size))
        own[d, 0] = combined[:, :tile]
        own[d, 1] = combined[:, tile:]

    def term_copy(index, d):
        if d == 0:
            return remote(
                packed_out.at[index], packed_in.at[index],
                term_sems.at[index, d, 0], term_sems.at[index, d, 1], targets[index],
            )
        return remote(
            outgoing.at[index, d, chosen(d)[1]], incoming.at[index, d],
            term_sems.at[index, d, 0], term_sems.at[index, d, 1], targets[index],
        )

    def mate_copy(index):
        return remote(
            outgoing.at[index, 0, 1], mate_incoming.at[index],
            mate_term_sems.at[index, 0], mate_term_sems.at[index, 1], targets[index],
        )

    def mirror_copy(d):
        to = mate if d == 0 else base + chosen(d)[0] * 2 + chosen(d)[1]
        return remote(
            mirror_out.at[d], mirror_in.at[d], mirror_sems.at[d, 0], mirror_sems.at[d, 1], to
        )

    def received(d):
        total = None
        for index in range(len(shifts)):
            term_copy(index, d).wait_recv()
            piece = (packed_in[index] if d == 0 else incoming[index, d]).astype(f32)
            total = piece if total is None else total + piece
        return total

    def put(j, value):
        columns = pl.ds(pl.multiple_of(j * tile, tile), tile)
        out[0, :, columns] = value[:tile]
        out[1, :, columns] = value[tile:]

    def mirrored(d):
        block = mirror_in[d]
        return jnp.concatenate([block[:tile].T.astype(f32), -block[tile:].T.astype(f32)], axis=0)

    for d in list(range(1, chips)) + [0]:
        second_products(d)
    for d in range(1, chips):
        other, pick = chosen(d)
        total = received(d)
        mirror_out[d] = total.astype(bf16)
        mirror_copy(d).start()
        put(other * 2 + pick, own[d, pick] + total)

    @pl.when(core == 0)
    def _():
        total = None
        for index in range(len(shifts)):
            mate_copy(index).wait_recv()
            piece = mate_incoming[index].astype(f32)
            total = piece if total is None else total + piece
        mirror_out[0] = total.astype(bf16)
        mirror_copy(0).start()
        put(chip * 2 + 1, own[0, 1] + total)

    for d in range(1, chips):
        source = lax.rem(chip + chips - d, chips)
        slot = chips - d
        same = jnp.where(source < chip, 1, 0)
        which = core * same + (1 - core) * (1 - same)
        mirror_copy(d).wait_recv()
        put(source * 2 + which, own[slot, which] + mirrored(d))

    packed = received(0)
    turned = packed.T
    below = lax.broadcasted_iota(jnp.int32, (tile, tile), 0) - lax.broadcasted_iota(
        jnp.int32, (tile, tile), 1
    )
    diagonal = jnp.concatenate(
        [
            jnp.where(below <= 0, packed, turned),
            jnp.where(below > 0, packed, jnp.where(below < 0, -turned, 0.0)),
        ],
        axis=0,
    )
    put(member, own[0, core] + diagonal)

    @pl.when(core == 1)
    def _():
        mirror_copy(0).wait_recv()
        put(chip * 2, own[0, 0] + mirrored(0))

    for copy in chip_copies.values():
        copy.wait_send()
    pair_copy.wait_send()
    for relay in relays:
        relay.wait_send()
    for index in range(len(shifts)):
        for d in range(chips):
            term_copy(index, d).wait_send()
    for d in range(1, chips):
        mirror_copy(d).wait_send()

    @pl.when(core == 0)
    def _():
        for index in range(len(shifts)):
            mate_copy(index).wait_send()
        mirror_copy(0).wait_send()


def body(green_function, couplings, phonon_modes, weights):
    _, tile, order = green_function.shape
    group = order // tile
    chips = group // 2
    bank_size = couplings.shape[0]
    stops, mode_count = phonon_modes.shape
    dims = (lax.axis_size("mom"), group, tile, order, bank_size, stops, mode_count)
    bf16, f32 = jnp.bfloat16, jnp.float32
    flops = 8 * bank_size * tile * order * order * 2
    dma = pltpu.SemaphoreType.DMA
    return pl.pallas_call(
        functools.partial(kernel, dims),
        out_shape=jax.ShapeDtypeStruct((2, tile, order), f32),
        in_specs=[pl.BlockSpec(memory_space=pltpu.HBM)] * 4,
        out_specs=pl.BlockSpec(memory_space=pltpu.VMEM),
        scratch_shapes=[
            pltpu.SMEM((stops, mode_count), jnp.int32),
            pltpu.SMEM((stops, mode_count), f32),
            pltpu.VMEM((group, 2, tile, order), bf16),
            pltpu.VMEM((bank_size, order, 2 * order), bf16),
            pltpu.VMEM((bank_size * tile, 2 * order), bf16),
            pltpu.VMEM((2, 2, tile, order), bf16),
            pltpu.VMEM((2, 2 * tile, 2 * order), bf16),
            pltpu.VMEM((bank_size, 2 * tile, 2 * order), bf16),
            pltpu.VMEM((chips, 2, 2 * tile, tile), f32),
            pltpu.VMEM((stops - 1, chips, 2, 2 * tile, tile), bf16),
            pltpu.VMEM((stops - 1, chips, 2 * tile, tile), bf16),
            pltpu.VMEM((stops - 1, tile, tile), bf16),
            pltpu.VMEM((stops - 1, tile, tile), bf16),
            pltpu.VMEM((stops - 1, 2 * tile, tile), bf16),
            pltpu.VMEM((chips, 2 * tile, tile), bf16),
            pltpu.VMEM((chips, 2 * tile, tile), bf16),
            dma((3,)),
            dma((bank_size, 2)),
            dma((2,)),
            dma((chips, chips, 2)),
            dma((chips, chips, 2)),
            dma((stops - 1, chips, 2)),
            dma((stops - 1, 2)),
            dma((chips, 2)),
        ],
        compiler_params=pltpu.CompilerParams(
            collective_id=0, has_side_effects=True, vmem_limit_bytes=63 * 2**20
        ),
        cost_estimate=pl.CostEstimate(flops=flops, bytes_accessed=10 * 2**20, transcendentals=0),
    )(green_function, couplings, phonon_modes, weights)


def solution(mesh):
    in_specs = (P(None, ("grp", "mom"), None), P(), P(), P())
    out_specs = P(None, ("grp", "mom"), None)
    return jax.shard_map(body, mesh=mesh, in_specs=in_specs, out_specs=out_specs, check_vma=False)
```
